32 devices in a mesh: cols: 8 (over y, x, core), rows: 4 (over z).
Axes of the slice: x: 2, y: 2, z: 4, core: 2. Of those that a mesh axis runs over, the one named last changes fastest.
Arguments:
- weight: float32 [8192, 26, 1024], P('rows', None, 'cols'), may hold values from -6 to 6
- factor_rows: bfloat16 [1024, 26, 1024], P('rows', None, 'cols'), may hold values from -0.1875 to 0.1875
- diag_inverse: float32 [8, 128, 128], replicated, may hold values from -1 to 2, as said below
- keep_codes: int32 [8192, 256], P('rows'), may hold values from 0 to 5
- block_order: int32 [8], replicated, may hold values from 0 to 7, each once
Outputs:
- pruned: float32 [8192, 26, 1024], P('rows', None, 'cols')
The draws below stay inside these ranges and needn't reach their ends.
Inputs may be any that keep to these rules, and one draw needn't show every extreme that they name: `block_order`: each entry of 0 to 7 appears once. `diag_inverse`: upper triangular with diagonal entries of 1 to 2.
All inputs are finite; a program needn't handle non-finite values.
Results may differ from the reference program's by a relative error of at most 0.0028.
Values may be sent and summed in bfloat16 or wider, within the bound.
A program may use at most 128 MiB of HBM per device.

```python
import jax
import jax.numpy as jnp
import numpy as np
from jax import lax

FF = 26624
BS = 128
BLOCKS = 8
R = 8192
LAPS = 26
N_COLS = 8


def draw_diag_inverse(key, part):
    first, second = jax.random.split(jax.random.fold_in(key, 11), 2)
    diagonal = jax.random.uniform(first, (BLOCKS, BS), jnp.float32, 1.0, 2.0)
    others = 0.4 * jax.random.normal(second, (BLOCKS, BS, BS), jnp.float32) / jnp.sqrt(jnp.float32(BS))
    upper = jnp.triu(others, 1)
    return upper + diagonal[:, :, None] * jnp.eye(BS, dtype=jnp.float32)[None, :, :]


def set_ends(entries, own_key, smallest, high):
    spot = [jax.random.randint(jax.random.fold_in(own_key, axis), (), 0, length) for axis, length in enumerate(entries.shape)]
    widest = entries.shape.index(max(entries.shape))
    beside = spot[:widest] + [(spot[widest] + 1) % entries.shape[widest]] + spot[widest + 1:]
    return entries.at[tuple(spot)].set(smallest).at[tuple(beside)].set(high)


def shard_levels(key, shape, pieces, low, high):
    def one(position, blocks):
        steps = jax.random.uniform(jax.random.fold_in(jax.random.fold_in(key, 6), position), (blocks,), jnp.float32, low / len(pieces), high / len(pieces))
        return jnp.repeat(jnp.exp(steps), shape[position] // blocks).reshape((-1,) + (1,) * (len(shape) - position - 1))

    loudness = one(*pieces[0])
    for cut in pieces[1:]:
        loudness = loudness * one(*cut)
    return loudness


def gaussian(stream_key, dims, scale, bound, pieces=(), kind=jnp.bfloat16):
    drawn = jax.random.normal(stream_key, dims, jnp.float32) * scale
    if len(pieces) > 0:
        drawn = shard_levels(stream_key, dims, pieces, -0.22, 0.18) * drawn
    return jnp.clip(drawn, min=-bound, max=bound).astype(kind)


def setup_inputs(seed: int = 0) -> dict:
    key_of = jax.random.split(jax.random.key(seed), 6)
    weight = gaussian(key_of[0], (R, LAPS, N_COLS * BS), 1.0, 6.0, ((0, 4), (2, 8)), jnp.float32)
    factor_rows = gaussian(key_of[1], (BLOCKS * BS, LAPS, N_COLS * BS), (BLOCKS * BS) ** -0.5, 0.1875, ((0, 4), (2, 8)))
    diag_inverse = draw_diag_inverse(jax.random.fold_in(key_of[5], 71), 0)
    keep_codes = set_ends(jax.random.randint(key_of[3], (R, BLOCKS * 32), 0, 6), jax.random.fold_in(key_of[3], 1), 0, 5).astype(jnp.int32)
    block_order = jax.random.permutation(key_of[4], BLOCKS).astype(jnp.int32)
    return dict(weight=weight, factor_rows=factor_rows, diag_inverse=diag_inverse, keep_codes=keep_codes, block_order=block_order)


pair_table = np.array([[1, 1, 0, 0], [1, 0, 1, 0], [1, 0, 0, 1], [0, 1, 1, 0], [0, 1, 0, 1], [0, 0, 1, 1]], dtype=np.float32)


def decode(codes):
    onehot = (codes[:, :, None] == jnp.arange(6, dtype=jnp.int32)).astype(jnp.float32)
    kept_mask = jnp.einsum("rgo,ok->rgk", onehot, jnp.asarray(pair_table, dtype=jnp.float32))
    return kept_mask.reshape(codes.shape[0], -1)


def reference(weight, factor_rows, diag_inverse, keep_codes, block_order):
    row_count = weight.shape[0]
    matrix = weight.reshape(row_count, FF)
    factor = factor_rows.reshape(BLOCKS * BS, FF)
    column_block = jnp.arange(FF, dtype=jnp.int32) // BS
    finished = jnp.zeros((FF // BS,), dtype=bool)
    for step_index in range(BLOCKS):
        block_now = block_order[step_index].astype(jnp.int32)
        col_start = (block_now * BS).astype(jnp.int32)
        block_vals = lax.dynamic_slice_in_dim(matrix, col_start, BS, 1)
        kept_mask = decode(lax.dynamic_slice_in_dim(keep_codes, (block_now * 32).astype(jnp.int32), 32, 1))
        errors_bf = jnp.dot(block_vals * (1.0 - kept_mask), diag_inverse[block_now], precision=lax.Precision.HIGHEST, preferred_element_type=jnp.float32).astype(jnp.bfloat16)
        finished = finished.at[block_now].set(True)
        factor_tile = lax.dynamic_slice_in_dim(factor, col_start, BS, 0)
        update_term = jnp.dot(errors_bf, factor_tile, preferred_element_type=jnp.float32)
        pending = jnp.logical_not(finished[column_block])
        matrix = jnp.where(pending[None, :], matrix - update_term, matrix)
        matrix = lax.dynamic_update_slice_in_dim(matrix, block_vals * kept_mask, col_start, 1)
    return matrix.reshape(weight.shape)
```

```python
import functools

import jax
import jax.numpy as jnp
from jax import lax
from jax.experimental import pallas as pl
from jax.experimental.pallas import tpu as pltpu
from jax.sharding import PartitionSpec as P

BLOCKS = 8
GROUP = 4


def keep_mask(codes, first_group, width):
    groups = codes.shape[1]
    row = lax.broadcasted_iota(jnp.int32, (groups, width), 0)
    column = lax.broadcasted_iota(jnp.int32, (groups, width), 1)
    pick = (row == first_group + column // GROUP).astype(jnp.float32).astype(jnp.bfloat16)
    spread_codes = jnp.dot(
        codes.astype(jnp.float32).astype(jnp.bfloat16), pick, preferred_element_type=jnp.float32
    )
    place = lax.broadcasted_iota(jnp.int32, (1, width), 1) % GROUP
    first = jnp.where(place < 2, 0.0, jnp.where(place == 2, 1.0, 2.0))
    second = jnp.where(place == 0, 1.0, jnp.where(place == 3, 4.0, 3.0))
    third = jnp.where(place == 0, 2.0, jnp.where(place == 1, 4.0, 5.0))
    hit = (spread_codes == first) | (spread_codes == second) | (spread_codes == third)
    return jnp.where(hit, 1.0, 0.0)


def chain_kernel(order_ref, block_ref, factor_ref, diag_ref, code_ref, error_ref, now):
    width = block_ref.shape[2]
    groups = code_ref.shape[1] // BLOCKS
    now[...] = block_ref[...]

    def step(s, carry):
        b = order_ref[s]
        kept = keep_mask(code_ref[...], b * groups, width)
        errors = jnp.dot(
            now[b] * (1.0 - kept),
            diag_ref[b],
            precision=lax.Precision.HIGHEST,
            preferred_element_type=jnp.float32,
        ).astype(jnp.bfloat16)
        start = pl.multiple_of(b * width, width)
        error_ref[:, pl.ds(start, width)] = errors
        for t in range(BLOCKS):
            now[t] -= jnp.dot(
                errors, factor_ref[t, pl.ds(start, width), :], preferred_element_type=jnp.float32
            )
        return carry

    lax.fori_loop(0, BLOCKS, step, 0)


def chain(order, blocks, factor, diag, codes):
    rows, width = blocks.shape[1:]
    whole = pl.BlockSpec(memory_space=pltpu.VMEM)
    return pl.pallas_call(
        chain_kernel,
        out_shape=jax.ShapeDtypeStruct((rows, BLOCKS * width), jnp.bfloat16),
        in_specs=[pl.BlockSpec(memory_space=pltpu.SMEM), whole, whole, whole, whole],
        out_specs=whole,
        scratch_shapes=[pltpu.VMEM(blocks.shape, jnp.float32)],
        compiler_params=pltpu.CompilerParams(vmem_limit_bytes=24 << 20),
        name="chain",
    )(order, blocks, factor, diag, codes)


def update_kernel(first, pair, rank_ref, error_ref, weight_ref, factor_ref, code_ref, *rest):
    out_ref = rest[-1]
    width = weight_ref.shape[2]

    def run(own):
        tiles = [factor_ref[i] for i in range(pair)]
        if own:
            depth = tiles[0].shape[0]
            column = rank_ref[BLOCKS]
            pruned = column < BLOCKS
            mine = jnp.where(pruned, rank_ref[jnp.minimum(column, BLOCKS - 1)], BLOCKS)
            block_of = lax.broadcasted_iota(jnp.int32, (depth, width), 0) // width
            position = jnp.zeros((depth, width), jnp.int32)
            for b in range(BLOCKS):
                position = jnp.where(block_of == b, rank_ref[b], position)
            tiles[0] = jnp.where(position < mine, tiles[0].astype(jnp.float32), 0.0).astype(jnp.bfloat16)
        tile = jnp.concatenate(tiles, axis=1) if pair > 1 else tiles[0]
        product = jnp.dot(error_ref[...], tile, preferred_element_type=jnp.float32)
        for i in range(pair):
            fresh = weight_ref[i] - product[:, i * width:(i + 1) * width]
            if own and i == 0:
                groups = code_ref.shape[1] // BLOCKS
                kept = keep_mask(code_ref[...], jnp.minimum(column, BLOCKS - 1) * groups, width)
                fresh = jnp.where(pruned, kept * fresh, fresh)
            out_ref[i] = fresh

    if first == 0:
        pl.when(pl.program_id(0) == 0)(lambda: run(True))
        pl.when(pl.program_id(0) > 0)(lambda: run(False))
    else:
        run(False)


def update(rank, errors, weight, factor, codes, first, so_far):
    laps, depth, width = factor.shape
    rows = weight.shape[1]
    pair = 2 if laps % 2 == 0 and first % 2 == 0 else 1
    if so_far is None:
        extra, extra_specs, aliases = [], [], {}
    else:
        extra, extra_specs, aliases = [so_far], [pl.BlockSpec(memory_space=pl.ANY)], {5: 0}
    return pl.pallas_call(
        functools.partial(update_kernel, first, pair),
        grid=(laps // pair,),
        out_shape=jax.ShapeDtypeStruct(weight.shape, weight.dtype),
        in_specs=[
            pl.BlockSpec(memory_space=pltpu.SMEM),
            pl.BlockSpec(memory_space=pltpu.VMEM),
            pl.BlockSpec((pair, rows, width), lambda i: (first // pair + i, 0, 0)),
            pl.BlockSpec((pair, depth, width), lambda i: (i, 0, 0)),
            pl.BlockSpec(memory_space=pltpu.VMEM),
        ] + extra_specs,
        out_specs=pl.BlockSpec((pair, rows, width), lambda i: (first // pair + i, 0, 0)),
        input_output_aliases=aliases,
        compiler_params=pltpu.CompilerParams(vmem_limit_bytes=40 << 20),
        cost_estimate=pl.CostEstimate(
            flops=2 * rows * depth * width * laps,
            bytes_accessed=laps * width * (8 * rows + 2 * depth),
            transcendentals=0,
        ),
        name="update",
    )(rank, errors, weight, factor, codes, *extra)


def body(weight, factor_rows, diag_inverse, keep_codes, block_order):
    columns = lax.axis_size("cols")
    column = lax.axis_index("cols").astype(jnp.int32)
    rows, laps, width = weight.shape
    part = rows // columns
    laps_first = weight.transpose(1, 0, 2)
    factor = factor_rows.transpose(1, 0, 2)

    spots = jnp.arange(BLOCKS, dtype=jnp.int32)
    rank = jnp.sum(jnp.where(block_order[None, :] == spots[:, None], spots[None, :], 0), axis=1)
    rank = jnp.concatenate([rank, column[None]]).astype(jnp.int32)

    factor_head = lax.all_gather(factor[0], ("cols", "rows"), axis=0, tiled=True)
    factor_head = factor_head.reshape(columns, -1, width)[:BLOCKS]
    head = lax.all_to_all(
        laps_first[0].reshape(columns, part, width), "cols", 0, 0, tiled=True
    )[:BLOCKS]
    my_codes = lax.dynamic_slice_in_dim(keep_codes, column * part, part, 0)
    my_errors = chain(block_order, head, factor_head, diag_inverse, my_codes)
    errors = lax.all_gather(my_errors, "cols", axis=0, tiled=True)

    half = max(2, (laps * 2 // 3) // 2 * 2)
    out = None
    for first, last in ((0, half), (half, laps)):
        chunk = lax.all_gather(factor[first:last], "rows", axis=1, tiled=True)
        out = update(rank, errors, laps_first, chunk, keep_codes, first, out)
    return out.transpose(1, 0, 2)


def solution(mesh):
    in_specs = (P("rows", None, "cols"), P("rows", None, "cols"), P(), P("rows", None), P())
    out_specs = P("rows", None, "cols")
    return jax.shard_map(body, mesh=mesh, in_specs=in_specs, out_specs=out_specs, check_vma=False)
```

```python
import functools

import jax
import jax.numpy as jnp
from jax import lax
from jax.experimental import pallas as pl
from jax.experimental.pallas import tpu as pltpu
from jax.sharding import PartitionSpec as P

BLOCKS = 8
GROUP = 4


def keep_mask(codes, first_group, width):
    groups = codes.shape[1]
    row = lax.broadcasted_iota(jnp.int32, (groups, width), 0)
    column = lax.broadcasted_iota(jnp.int32, (groups, width), 1)
    pick = (row == first_group + column // GROUP).astype(jnp.float32).astype(jnp.bfloat16)
    spread_codes = jnp.dot(
        codes.astype(jnp.float32).astype(jnp.bfloat16), pick, preferred_element_type=jnp.float32
    )
    place = lax.broadcasted_iota(jnp.int32, (1, width), 1) % GROUP
    first = jnp.where(place < 2, 0.0, jnp.where(place == 2, 1.0, 2.0))
    second = jnp.where(place == 0, 1.0, jnp.where(place == 3, 4.0, 3.0))
    third = jnp.where(place == 0, 2.0, jnp.where(place == 1, 4.0, 5.0))
    hit = (spread_codes == first) | (spread_codes == second) | (spread_codes == third)
    return jnp.where(hit, 1.0, 0.0)


def chunk_ends(laps):
    bounds = [(0, 1)] if laps else []
    at = 1
    while at < laps:
        left = laps - at
        size = 6 if left >= 15 else 4 if left >= 7 else min(left, 3)
        bounds.append((at, at + size))
        at += size
    return bounds


def prune_kernel(
    n_rows, n_cols, order_ref, weight_ref, factor_ref, diag_ref, code_ref, out_ref,
    gathered, errors, heads, head_factor, by_step,
    factor_send, factor_recv, head_send, head_recv,
    spread_send, spread_recv, local_sem,
):
    laps, rows, width = weight_ref.shape
    depth = factor_ref.shape[1]
    part = rows // n_cols
    pairs = n_cols // 2
    groups = code_ref.shape[1] // BLOCKS
    bounds = chunk_ends(laps)
    count = len(bounds)
    z = lax.axis_index("rows")
    c = lax.axis_index("cols")
    partner = c + 1 - 2 * lax.rem(c, 2)

    def around(k):
        return lax.rem(c + k + n_cols, n_cols)

    def cut(index, size):
        return pl.ds(pl.multiple_of(index * size, size), size)

    barrier = pltpu.get_barrier_semaphore()
    for k in range(1, n_cols):
        pl.semaphore_signal(
            barrier, inc=1, device_id={"cols": around(k)}, device_id_type=pl.DeviceIdType.MESH
        )

    @pl.when(z > 0)
    def _():
        pl.semaphore_signal(
            barrier, inc=1, device_id={"rows": z - 1}, device_id_type=pl.DeviceIdType.MESH
        )

    @pl.when(z < n_rows - 1)
    def _():
        pl.semaphore_signal(
            barrier, inc=1, device_id={"rows": z + 1}, device_id_type=pl.DeviceIdType.MESH
        )

    below = jnp.where(z > 0, 1, 0)
    above = jnp.where(z < n_rows - 1, 1, 0)
    pl.semaphore_wait(barrier, n_cols - 1 + below + above)

    def factor_copy(q, source, up, own):
        low, high = bounds[q]
        place = gathered.at[pl.ds(low, high - low), cut(source, depth), :]
        return pltpu.make_async_remote_copy(
            src_ref=factor_ref.at[pl.ds(low, high - low)] if own else place,
            dst_ref=place,
            send_sem=factor_send.at[up, source, q],
            recv_sem=factor_recv.at[source, q],
            device_id={"rows": z + 1 if up else z - 1},
            device_id_type=pl.DeviceIdType.MESH,
        )

    def own(q):
        if q < count:
            pl.when(z > 0)(lambda: factor_copy(q, z, 0, True).start())
            pl.when(z < n_rows - 1)(lambda: factor_copy(q, z, 1, True).start())

    def hop(q, k):
        if q >= count or k >= n_rows:
            return

        @pl.when(z + k < n_rows)
        def _():
            factor_copy(q, z + k, 0, False).wait_recv()
            pl.when(z > 0)(lambda: factor_copy(q, z + k, 0, False).start())

        @pl.when(z - k >= 0)
        def _():
            factor_copy(q, z - k, 1, False).wait_recv()
            pl.when(z < n_rows - 1)(lambda: factor_copy(q, z - k, 1, False).start())

    def hops(q, first=1):
        for k in range(first, n_rows):
            hop(q, k)

    def head_copy(target, source):
        return pltpu.make_async_remote_copy(
            src_ref=weight_ref.at[0, cut(target, part), :],
            dst_ref=heads.at[source],
            send_sem=head_send.at[target],
            recv_sem=head_recv.at[source],
            device_id={"cols": target},
            device_id_type=pl.DeviceIdType.MESH,
        )

    def spread_copy(kind, source, target, slot):
        if kind == 0:
            block = head_factor.at[source]
        else:
            block = errors.at[cut(source, part), :]
        return pltpu.make_async_remote_copy(
            src_ref=block,
            dst_ref=block,
            send_sem=spread_send.at[kind, slot],
            recv_sem=spread_recv.at[kind, source],
            device_id={"cols": target},
            device_id_type=pl.DeviceIdType.MESH,
        )

    def spread_start(kind):
        for k in range(1, pairs):
            spread_copy(kind, c, around(2 * k), k).start()
        spread_copy(kind, c, partner, 0).start()

    def spread_forward(kind):
        for k in range(1, pairs):
            source = around(-2 * k)
            spread_copy(kind, source, partner, pairs + k).wait_recv()
            spread_copy(kind, source, partner, pairs + k).start()

    def spread_finish(kind):
        spread_copy(kind, partner, partner, 0).wait_recv()
        for k in range(1, pairs):
            spread_copy(kind, lax.rem(partner - 2 * k + n_cols, n_cols), partner, pairs + k).wait_recv()

    own(0)
    for k in range(1, n_cols):
        head_copy(around(k), c).start()
    own(1)
    own_head = pltpu.make_async_copy(weight_ref.at[0, cut(c, part), :], heads.at[c], local_sem.at[0])
    own_head.start()
    own_factor = pltpu.make_async_copy(factor_ref, gathered.at[:, cut(z, depth), :], local_sem.at[1])
    own_factor.start()
    fetch = pltpu.make_async_copy(weight_ref, out_ref, local_sem.at[2])
    fetch.start()

    hops(0)
    own_factor.wait()
    own(2)
    head_factor[c] = gathered[0].reshape(BLOCKS, width, width)
    spread_start(0)
    own_head.wait()
    for k in range(1, n_cols):
        head_copy(c, around(-k)).wait_recv()
    hop(1, 1)
    spread_forward(0)
    spread_finish(0)
    hop(1, 2)

    my_codes = code_ref.at[cut(c, part), :]

    def step(s, carry):
        b = order_ref[s]
        kept = keep_mask(my_codes[...], b * groups, width)
        fresh = jnp.dot(
            heads[b] * (1.0 - kept),
            diag_ref[b],
            precision=lax.Precision.HIGHEST,
            preferred_element_type=jnp.float32,
        ).astype(jnp.bfloat16)
        by_step[s] = fresh
        for t in range(BLOCKS):
            heads[t] = heads[t] - jnp.dot(fresh, head_factor[t, b], preferred_element_type=jnp.float32)
        return carry

    lax.fori_loop(0, BLOCKS, step, 0)

    rank = []
    for b in range(BLOCKS):
        at = 0
        for s in range(BLOCKS):
            at = at + jnp.where(order_ref[s] == b, s, 0)
        at = jnp.minimum(at, BLOCKS - 1)
        rank.append(at)
        errors[cut(c, part), b * width:(b + 1) * width] = by_step[at]

    spread_start(1)
    own(3)
    hops(1, 3)
    hop(2, 1)
    spread_forward(1)
    hop(2, 2)
    spread_finish(1)
    own(4)
    hops(2, 3)
    hop(3, 1)
    fetch.wait()

    tile_rows = min(rows, 512)

    def by_rows(work):
        lax.fori_loop(0, rows // tile_rows, lambda i, carry: work(cut(i, tile_rows)) or carry, 0)

    def first_lap():
        column = jnp.minimum(c, BLOCKS - 1)
        pruned = c < BLOCKS
        mine = BLOCKS
        for b in range(BLOCKS):
            mine = jnp.where(c == b, rank[b], mine)
        block_of = lax.broadcasted_iota(jnp.int32, (BLOCKS * width, width), 0) // width
        position = jnp.zeros((BLOCKS * width, width), jnp.int32)
        for b in range(BLOCKS):
            position = jnp.where(block_of == b, rank[b], position)
        tile = jnp.where(position < mine, gathered[0].astype(jnp.float32), 0.0).astype(jnp.bfloat16)

        def work(at):
            product = jnp.dot(errors[at, :], tile, preferred_element_type=jnp.float32)
            fresh = out_ref[0, at, :] - product
            kept = keep_mask(code_ref[at, :], column * groups, width)
            out_ref[0, at, :] = jnp.where(pruned, kept * fresh, fresh)

        by_rows(work)

    def laps_at(lap, many):
        tile = [gathered[lap + i] for i in range(many)]
        tile = jnp.concatenate(tile, axis=1) if many > 1 else tile[0]

        def work(at):
            product = jnp.dot(errors[at, :], tile, preferred_element_type=jnp.float32)
            for i in range(many):
                out_ref[lap + i, at, :] = out_ref[lap + i, at, :] - product[:, i * width:(i + 1) * width]

        by_rows(work)

    def compute(q):
        low, high = bounds[q]
        if q == 0:
            first_lap()
            return
        twos = (high - low) // 2
        lax.fori_loop(0, twos, lambda i, carry: laps_at(low + 2 * i, 2) or carry, 0)
        if (high - low) % 2:
            laps_at(high - 1, 1)

    compute(0)
    hop(3, 2)
    compute(1)
    hops(3, 3)
    own(5)
    hop(4, 1)
    compute(2)
    for q in range(3, count):
        own(q + 3)
        hops(q + 1, 2)
        hop(q + 2, 1)
        compute(q)

    for q in range(count):
        for source in range(n_rows):
            pl.when((z > 0) & (z <= source))(lambda: factor_copy(q, source, 0, False).wait_send())
            pl.when((z < n_rows - 1) & (z >= source))(lambda: factor_copy(q, source, 1, False).wait_send())
    for k in range(1, n_cols):
        head_copy(around(k), c).wait_send()
    for kind in range(2):
        for slot in range(2 * pairs):
            if slot != pairs:
                spread_copy(kind, c, partner, slot).wait_send()


def store_kernel(kept_ref, out_ref, sems):
    laps = kept_ref.shape[0]
    copies = [pltpu.make_async_copy(kept_ref.at[l], out_ref.at[l], sems.at[l]) for l in range(laps)]
    for copy in copies:
        copy.start()
    for copy in copies:
        copy.wait()


def store(kept):
    return pl.pallas_call(
        store_kernel,
        out_shape=jax.ShapeDtypeStruct(kept.shape, kept.dtype),
        in_specs=[pl.BlockSpec(memory_space=pltpu.VMEM)],
        out_specs=pl.BlockSpec(memory_space=pl.ANY),
        scratch_shapes=[pltpu.SemaphoreType.DMA((kept.shape[0],))],
        compiler_params=pltpu.CompilerParams(vmem_limit_bytes=1 << 20),
        name="store",
    )(kept)


def body(weight, factor_rows, diag_inverse, keep_codes, block_order):
    n_rows, n_cols = lax.axis_size("rows"), lax.axis_size("cols")
    rows, laps, width = weight.shape
    part = rows // n_cols
    depth = factor_rows.shape[0] * n_rows
    count = len(chunk_ends(laps))
    anywhere = pl.BlockSpec(memory_space=pl.ANY)
    inside = pl.BlockSpec(memory_space=pltpu.VMEM)
    dma = pltpu.SemaphoreType.DMA
    out = pl.pallas_call(
        functools.partial(prune_kernel, n_rows, n_cols),
        out_shape=pltpu.VMEM((laps, rows, width), jnp.float32),
        in_specs=[pl.BlockSpec(memory_space=pltpu.SMEM), anywhere, anywhere, inside, inside],
        out_specs=inside,
        scratch_shapes=[
            pltpu.VMEM((laps, depth, width), jnp.bfloat16),
            pltpu.VMEM((rows, BLOCKS * width), jnp.bfloat16),
            pltpu.VMEM((n_cols, part, width), jnp.float32),
            pltpu.VMEM((n_cols, BLOCKS, width, width), jnp.bfloat16),
            pltpu.VMEM((BLOCKS, part, width), jnp.bfloat16),
            dma((2, n_rows, count)),
            dma((n_rows, count)),
            dma((n_cols,)),
            dma((n_cols,)),
            dma((2, n_cols)),
            dma((2, n_cols)),
            dma((3,)),
        ],
        compiler_params=pltpu.CompilerParams(
            collective_id=0, has_side_effects=True, vmem_limit_bytes=30 << 20
        ),
        cost_estimate=pl.CostEstimate(
            flops=2 * rows * depth * width * laps,
            bytes_accessed=laps * width * (8 * rows + 2 * depth),
            transcendentals=0,
        ),
        name="prune",
    )(
        block_order,
        weight.transpose(1, 0, 2),
        factor_rows.transpose(1, 0, 2),
        diag_inverse,
        keep_codes,
    )
    return store(out).transpose(1, 0, 2)


def solution(mesh):
    in_specs = (P("rows", None, "cols"), P("rows", None, "cols"), P(), P("rows", None), P())
    out_specs = P("rows", None, "cols")
    return jax.shard_map(body, mesh=mesh, in_specs=in_specs, out_specs=out_specs, check_vma=False)
```

```python
import functools

import jax
import jax.numpy as jnp
from jax import lax
from jax.experimental import pallas as pl
from jax.experimental.pallas import tpu as pltpu
from jax.sharding import PartitionSpec as P

BLOCKS = 8
GROUP = 4


def keep_mask(codes, first_group, width):
    groups = codes.shape[1]
    row = lax.broadcasted_iota(jnp.int32, (groups, width), 0)
    column = lax.broadcasted_iota(jnp.int32, (groups, width), 1)
    pick = (row == first_group + column // GROUP).astype(jnp.float32).astype(jnp.bfloat16)
    spread_codes = jnp.dot(
        codes.astype(jnp.float32).astype(jnp.bfloat16), pick, preferred_element_type=jnp.float32
    )
    place = lax.broadcasted_iota(jnp.int32, (1, width), 1) % GROUP
    first = jnp.where(place < 2, 0.0, jnp.where(place == 2, 1.0, 2.0))
    second = jnp.where(place == 0, 1.0, jnp.where(place == 3, 4.0, 3.0))
    third = jnp.where(place == 0, 2.0, jnp.where(place == 1, 4.0, 5.0))
    hit = (spread_codes == first) | (spread_codes == second) | (spread_codes == third)
    return jnp.where(hit, 1.0, 0.0)


def chunk_ends(laps):
    bounds = [(0, 1)] if laps else []
    at = 1
    while at < laps:
        left = laps - at
        size = 6 if left >= 15 else 4 if left >= 7 else min(left, 3)
        bounds.append((at, at + size))
        at += size
    return bounds


def prune_kernel(
    n_rows, n_cols, order_ref, weight_ref, factor_ref, diag_ref, code_ref, out_ref,
    gathered, errors, heads, head_factor, by_step,
    factor_send, factor_recv, head_send, head_recv,
    spread_send, spread_recv, local_sem,
):
    laps, rows, width = weight_ref.shape
    depth = factor_ref.shape[1]
    part = rows // n_cols
    pairs = n_cols // 2
    groups = code_ref.shape[1] // BLOCKS
    bounds = chunk_ends(laps)
    count = len(bounds)
    z = lax.axis_index("rows")
    c = lax.axis_index("cols")
    partner = c + 1 - 2 * lax.rem(c, 2)

    def around(k):
        return lax.rem(c + k + n_cols, n_cols)

    def cut(index, size):
        return pl.ds(pl.multiple_of(index * size, size), size)

    barrier = pltpu.get_barrier_semaphore()
    for k in range(1, n_cols):
        pl.semaphore_signal(
            barrier, inc=1, device_id={"cols": around(k)}, device_id_type=pl.DeviceIdType.MESH
        )

    @pl.when(z > 0)
    def _():
        pl.semaphore_signal(
            barrier, inc=1, device_id={"rows": z - 1}, device_id_type=pl.DeviceIdType.MESH
        )

    @pl.when(z < n_rows - 1)
    def _():
        pl.semaphore_signal(
            barrier, inc=1, device_id={"rows": z + 1}, device_id_type=pl.DeviceIdType.MESH
        )

    below = jnp.where(z > 0, 1, 0)
    above = jnp.where(z < n_rows - 1, 1, 0)
    pl.semaphore_wait(barrier, n_cols - 1 + below + above)

    def factor_copy(q, source, up, own):
        low, high = bounds[q]
        place = gathered.at[pl.ds(low, high - low), cut(source, depth), :]
        return pltpu.make_async_remote_copy(
            src_ref=factor_ref.at[pl.ds(low, high - low)] if own else place,
            dst_ref=place,
            send_sem=factor_send.at[up, source, q],
            recv_sem=factor_recv.at[source, q],
            device_id={"rows": z + 1 if up else z - 1},
            device_id_type=pl.DeviceIdType.MESH,
        )

    def own(q):
        if q < count:
            pl.when(z > 0)(lambda: factor_copy(q, z, 0, True).start())
            pl.when(z < n_rows - 1)(lambda: factor_copy(q, z, 1, True).start())

    def hop(q, k):
        if q >= count or k >= n_rows:
            return

        @pl.when(z + k < n_rows)
        def _():
            factor_copy(q, z + k, 0, False).wait_recv()
            pl.when(z > 0)(lambda: factor_copy(q, z + k, 0, False).start())

        @pl.when(z - k >= 0)
        def _():
            factor_copy(q, z - k, 1, False).wait_recv()
            pl.when(z < n_rows - 1)(lambda: factor_copy(q, z - k, 1, False).start())

    def middle(q):
        for k in range(2, n_rows - 1):
            hop(q, k)

    def last(q):
        if n_rows > 2:
            hop(q, n_rows - 1)

    def head_copy(target, source):
        return pltpu.make_async_remote_copy(
            src_ref=weight_ref.at[0, cut(target, part), :],
            dst_ref=heads.at[source],
            send_sem=head_send.at[target],
            recv_sem=head_recv.at[source],
            device_id={"cols": target},
            device_id_type=pl.DeviceIdType.MESH,
        )

    def spread_copy(kind, source, target, slot):
        if kind == 0:
            block = head_factor.at[source]
        else:
            block = errors.at[cut(source, part), :]
        return pltpu.make_async_remote_copy(
            src_ref=block,
            dst_ref=block,
            send_sem=spread_send.at[kind, slot],
            recv_sem=spread_recv.at[kind, source],
            device_id={"cols": target},
            device_id_type=pl.DeviceIdType.MESH,
        )

    def spread_start(kind):
        for k in range(1, pairs):
            spread_copy(kind, c, around(2 * k), k).start()
        spread_copy(kind, c, partner, 0).start()

    def spread_forward(kind):
        for k in range(1, pairs):
            source = around(-2 * k)
            spread_copy(kind, source, partner, pairs + k).wait_recv()
            spread_copy(kind, source, partner, pairs + k).start()

    def spread_finish(kind):
        spread_copy(kind, partner, partner, 0).wait_recv()
        for k in range(1, pairs):
            spread_copy(kind, lax.rem(partner - 2 * k + n_cols, n_cols), partner, pairs + k).wait_recv()

    own(0)
    for k in range(1, n_cols):
        head_copy(around(k), c).start()
    own_head = pltpu.make_async_copy(weight_ref.at[0, cut(c, part), :], heads.at[c], local_sem.at[0])
    own_head.start()
    own_factor = pltpu.make_async_copy(factor_ref, gathered.at[:, cut(z, depth), :], local_sem.at[1])
    own_factor.start()
    fetch = pltpu.make_async_copy(weight_ref, out_ref, local_sem.at[2])
    fetch.start()

    hop(0, 1)
    middle(0)
    last(0)
    own(1)
    own(2)
    own(3)
    own_factor.wait()
    head_factor[c] = gathered[0].reshape(BLOCKS, width, width)
    spread_start(0)
    own_head.wait()
    for k in range(1, n_cols):
        head_copy(c, around(-k)).wait_recv()
    spread_forward(0)
    hop(1, 1)
    spread_finish(0)

    my_codes = code_ref.at[cut(c, part), :]

    def step(s, carry):
        b = order_ref[s]
        kept = keep_mask(my_codes[...], b * groups, width)
        fresh = jnp.dot(
            heads[b] * (1.0 - kept),
            diag_ref[b],
            precision=lax.Precision.HIGHEST,
            preferred_element_type=jnp.float32,
        ).astype(jnp.bfloat16)
        by_step[s] = fresh
        for t in range(BLOCKS):
            heads[t] = heads[t] - jnp.dot(fresh, head_factor[t, b], preferred_element_type=jnp.float32)
        return carry

    lax.fori_loop(0, BLOCKS, step, 0)

    rank = []
    for b in range(BLOCKS):
        at = 0
        for s in range(BLOCKS):
            at = at + jnp.where(order_ref[s] == b, s, 0)
        at = jnp.minimum(at, BLOCKS - 1)
        rank.append(at)
        errors[cut(c, part), b * width:(b + 1) * width] = by_step[at]

    spread_start(1)
    hop(2, 1)
    own(4)
    middle(1)
    hop(3, 1)
    spread_forward(1)
    own(5)
    middle(2)
    spread_finish(1)
    last(1)
    fetch.wait()

    tile_rows = min(rows, 512)

    def by_rows(work):
        lax.fori_loop(0, rows // tile_rows, lambda i, carry: work(cut(i, tile_rows)) or carry, 0)

    def first_lap():
        column = jnp.minimum(c, BLOCKS - 1)
        pruned = c < BLOCKS
        mine = BLOCKS
        for b in range(BLOCKS):
            mine = jnp.where(c == b, rank[b], mine)
        block_of = lax.broadcasted_iota(jnp.int32, (BLOCKS * width, width), 0) // width
        position = jnp.zeros((BLOCKS * width, width), jnp.int32)
        for b in range(BLOCKS):
            position = jnp.where(block_of == b, rank[b], position)
        tile = jnp.where(position < mine, gathered[0].astype(jnp.float32), 0.0).astype(jnp.bfloat16)

        def work(at):
            product = jnp.dot(errors[at, :], tile, preferred_element_type=jnp.float32)
            fresh = out_ref[0, at, :] - product
            kept = keep_mask(code_ref[at, :], column * groups, width)
            out_ref[0, at, :] = jnp.where(pruned, kept * fresh, fresh)

        by_rows(work)

    def laps_at(lap, many):
        tile = [gathered[lap + i] for i in range(many)]
        tile = jnp.concatenate(tile, axis=1) if many > 1 else tile[0]

        def work(at):
            product = jnp.dot(errors[at, :], tile, preferred_element_type=jnp.float32)
            for i in range(many):
                out_ref[lap + i, at, :] = out_ref[lap + i, at, :] - product[:, i * width:(i + 1) * width]

        by_rows(work)

    def compute(q):
        low, high = bounds[q]
        if q == 0:
            first_lap()
            return
        twos = (high - low) // 2
        lax.fori_loop(0, twos, lambda i, carry: laps_at(low + 2 * i, 2) or carry, 0)
        if (high - low) % 2:
            laps_at(high - 1, 1)

    compute(0)
    compute(1)
    own(6)
    middle(3)
    hop(4, 1)
    last(2)
    compute(2)
    for q in range(3, count):
        own(q + 4)
        middle(q + 1)
        hop(q + 2, 1)
        last(q)
        compute(q)

    for q in range(count):
        for source in range(n_rows):
            pl.when((z > 0) & (z <= source))(lambda: factor_copy(q, source, 0, False).wait_send())
            pl.when((z < n_rows - 1) & (z >= source))(lambda: factor_copy(q, source, 1, False).wait_send())
    for k in range(1, n_cols):
        head_copy(around(k), c).wait_send()
    for kind in range(2):
        for slot in range(2 * pairs):
            if slot != pairs:
                spread_copy(kind, c, partner, slot).wait_send()


def store_kernel(kept_ref, out_ref, sems):
    laps = kept_ref.shape[0]
    copies = [pltpu.make_async_copy(kept_ref.at[l], out_ref.at[l], sems.at[l]) for l in range(laps)]
    for copy in copies:
        copy.start()
    for copy in copies:
        copy.wait()


def store(kept):
    return pl.pallas_call(
        store_kernel,
        out_shape=jax.ShapeDtypeStruct(kept.shape, kept.dtype),
        in_specs=[pl.BlockSpec(memory_space=pltpu.VMEM)],
        out_specs=pl.BlockSpec(memory_space=pl.ANY),
        scratch_shapes=[pltpu.SemaphoreType.DMA((kept.shape[0],))],
        compiler_params=pltpu.CompilerParams(vmem_limit_bytes=1 << 20),
        name="store",
    )(kept)


def body(weight, factor_rows, diag_inverse, keep_codes, block_order):
    n_rows, n_cols = lax.axis_size("rows"), lax.axis_size("cols")
    rows, laps, width = weight.shape
    part = rows // n_cols
    depth = factor_rows.shape[0] * n_rows
    count = len(chunk_ends(laps))
    anywhere = pl.BlockSpec(memory_space=pl.ANY)
    inside = pl.BlockSpec(memory_space=pltpu.VMEM)
    dma = pltpu.SemaphoreType.DMA
    out = pl.pallas_call(
        functools.partial(prune_kernel, n_rows, n_cols),
        out_shape=pltpu.VMEM((laps, rows, width), jnp.float32),
        in_specs=[pl.BlockSpec(memory_space=pltpu.SMEM), anywhere, anywhere, inside, inside],
        out_specs=inside,
        scratch_shapes=[
            pltpu.VMEM((laps, depth, width), jnp.bfloat16),
            pltpu.VMEM((rows, BLOCKS * width), jnp.bfloat16),
            pltpu.VMEM((n_cols, part, width), jnp.float32),
            pltpu.VMEM((n_cols, BLOCKS, width, width), jnp.bfloat16),
            pltpu.VMEM((BLOCKS, part, width), jnp.bfloat16),
            dma((2, n_rows, count)),
            dma((n_rows, count)),
            dma((n_cols,)),
            dma((n_cols,)),
            dma((2, n_cols)),
            dma((2, n_cols)),
            dma((3,)),
        ],
        compiler_params=pltpu.CompilerParams(
            collective_id=0, has_side_effects=True, vmem_limit_bytes=30 << 20
        ),
        cost_estimate=pl.CostEstimate(
            flops=2 * rows * depth * width * laps,
            bytes_accessed=laps * width * (8 * rows + 2 * depth),
            transcendentals=0,
        ),
        name="prune",
    )(
        block_order,
        weight.transpose(1, 0, 2),
        factor_rows.transpose(1, 0, 2),
        diag_inverse,
        keep_codes,
    )
    return store(out).transpose(1, 0, 2)


def solution(mesh):
    in_specs = (P("rows", None, "cols"), P("rows", None, "cols"), P(), P("rows", None), P())
    out_specs = P("rows", None, "cols")
    return jax.shard_map(body, mesh=mesh, in_specs=in_specs, out_specs=out_specs, check_vma=False)
```
